32 devices in a mesh: row: 4 (over y, x), col: 8 (over z, core).
Axes of the slice: x: 2, y: 2, z: 4, core: 2. Of those that a mesh axis runs over, the one named last changes fastest.
Arguments:
- tokens: bfloat16 [2048, 1536], P('row', 'col'), may hold values from -6 to 6
- weight: bfloat16 [1536, 49152], P('row', 'col'), may hold values from -0.15625 to 0.15625
- counts: int32 [4], P('row'), may hold values from 1 to 512
- owner: int32 [4], replicated, may hold values from 0 to 3, each once
Outputs:
- window_product: float32 [2048, 49152], P('row', 'col')
The draws below stay inside these ranges and needn't reach their ends.
Inputs may be any that keep to these rules, and one draw needn't show every extreme that they name: `owner`: each number occurs once.
All inputs are finite; a program needn't handle non-finite values.
Results may differ from the reference program's by a relative error of at most 0.0003.
Values may be sent and summed in bfloat16 or wider, within the bound.
A program may use at most 128 MiB of HBM per device.

```python
import jax
import jax.numpy as jnp

FF = 49152
PANEL = 384
NPAN = 4
TR = 512
K = 1536
TOKENS = 2048
N_ROW = 4


def plant(drawn, own_key, low, largest):
    place = [jax.random.randint(jax.random.fold_in(own_key, axis), (), 0, length) for axis, length in enumerate(drawn.shape)]
    main_axis = drawn.shape.index(max(drawn.shape))
    next_to = place[:main_axis] + [(place[main_axis] + 1) % drawn.shape[main_axis]] + place[main_axis + 1:]
    return drawn.at[tuple(place)].set(low).at[tuple(next_to)].set(largest)


def shard_levels(own_key, extent, pieces, smallest, largest):
    factor_of, own = 1.0, jax.random.fold_in(own_key, 6)
    for axis_at, shards_of in pieces:
        steps = jnp.exp(jax.random.uniform(jax.random.fold_in(own, axis_at), (shards_of,), jnp.float32, smallest / len(pieces), largest / len(pieces)))
        factor_of = factor_of * jnp.repeat(steps, extent[axis_at] // shards_of).reshape([-1 if axis == axis_at else 1 for axis in range(len(extent))])
    return factor_of


def centred(rng, shape, deviation, most, split=(), held_as=jnp.bfloat16):
    drawn = jax.random.normal(rng, shape, jnp.float32) * deviation
    if len(split) > 0:
        drawn = shard_levels(rng, shape, split, -0.22, 0.18) * drawn
    return jnp.clip(drawn, min=-most, max=most).astype(held_as)


def setup_inputs(seed: int = 0) -> dict:
    keys = jax.random.split(jax.random.key(seed), 5)
    tokens = centred(keys[0], (TOKENS, K), 1.0, 6.0, ((0, 4), (1, 8)))
    weight = centred(keys[1], (K, FF), K ** -0.5, 0.15625, ((0, 4), (1, 8)))
    counts = plant(jax.random.randint(keys[2], (N_ROW,), 1, TR + 1), jax.random.fold_in(keys[2], 1), 1, TR).astype(jnp.int32)
    owner = jax.random.permutation(keys[3], NPAN).astype(jnp.int32)
    return dict(tokens=tokens, weight=weight, counts=counts, owner=owner)


def reference(tokens, weight, counts, owner):
    slotted = tokens.reshape(TOKENS, NPAN, PANEL)
    aligned = jnp.take(slotted, owner, axis=1).reshape(TOKENS, NPAN * PANEL)
    product = jnp.dot(aligned, weight, preferred_element_type=jnp.float32)
    position = jnp.arange(TOKENS, dtype=jnp.int32)
    within = position % TR
    block_index = position // TR
    kept = within < counts[block_index]
    return jnp.where(kept[:, None], product, jnp.float32(0.0))
```

```python
import functools

import jax
import jax.numpy as jnp
from jax import lax
from jax.experimental import pallas as pl
from jax.experimental.pallas import tpu as pltpu
from jax.sharding import PartitionSpec as P

MESH = pl.DeviceIdType.MESH
GROUPS = 8


def align_panels(gathered, owner):
    row_count = gathered.shape[0]
    panels = owner.shape[0]
    slotted = gathered.reshape(row_count, panels, gathered.shape[1] // panels)
    return jnp.take(slotted, owner, axis=1).reshape(row_count, gathered.shape[1])


def per_device_general(tokens, weight, counts, owner):
    row_count = tokens.shape[0]
    aligned = align_panels(lax.all_gather(tokens, "col", axis=1, tiled=True), owner)
    gathered_w = lax.all_gather(weight, "row", axis=0, tiled=True)
    product = jnp.dot(aligned, gathered_w, preferred_element_type=jnp.float32)
    token_limit = counts[0]
    kept = jnp.arange(row_count, dtype=jnp.int32) < token_limit
    return jnp.where(kept[:, None], product, jnp.float32(0.0))


def kernel(
    orients, nc, cw,
    counts, owner, tok_in, w_in, out,
    tokb, al, wb, qb, qs, rb, rs, ob,
    tl_sem, ta_s, ta_r, tb_s, tb_r,
    wl_sem, px_s, px_r, py_s, py_r, fy_s, fy_r, ox_s, ox_r, os_s, os_r, ol_sem,
):
    rows, piece = tok_in.shape
    panel = w_in.shape[0]
    half = nc * cw
    row, col = lax.axis_index("row"), lax.axis_index("col")
    y, x = row // 2, row % 2
    z, core = col // 2, col % 2
    z_hi, z_lo = z // 2, z % 2
    x_dev = (y * 2 + (1 - x), col)
    y_dev = ((1 - y) * 2 + x, col)
    z1_dev = (row, (z_hi * 2 + (1 - z_lo)) * 2 + core)
    z2_dev = (row, ((1 - z_hi) * 2 + z_lo) * 2 + core)
    c_dev = (row, z * 2 + (1 - core))
    peers = (x_dev, y_dev, z1_dev, z2_dev, c_dev)

    barrier = pltpu.get_barrier_semaphore()
    for peer in peers:
        pl.semaphore_signal(barrier, inc=1, device_id=peer, device_id_type=MESH)
    pl.semaphore_wait(barrier, len(peers))

    def remote(src, dst, send, recv, dev):
        return pltpu.make_async_remote_copy(
            src_ref=src, dst_ref=dst, send_sem=send, recv_sem=recv,
            device_id=dev, device_id_type=MESH)

    a_dev = (x_dev, y_dev)
    b_dev = (y_dev, x_dev)
    side = (x, y)

    def cols(o, s, k):
        return pl.ds(pl.multiple_of(orients.index(o) * 2 * half + s * half + k * cw, 128), cw)

    def at(o, k):
        return orients.index(o) * nc + k

    def px(o, k):
        g = at(o, k)
        return remote(w_in.at[:, cols(o, 1 - side[o], k)], wb.at[g, 1 + o],
                      px_s.at[g], px_r.at[g], a_dev[o])

    def py(o, k):
        g = at(o, k)
        return remote(w_in.at[:, cols(o, side[o], k)], wb.at[g, 2 - o],
                      py_s.at[g], py_r.at[g], b_dev[o])

    def fy(o, k):
        g = at(o, k)
        return remote(wb.at[g, 1 + o], wb.at[g, 3], fy_s.at[g], fy_r.at[g], b_dev[o])

    def wl(o, k):
        g = at(o, k)
        return pltpu.make_async_copy(
            w_in.at[:, cols(o, side[o], k)], wb.at[g, 0], wl_sem.at[g])

    def ox(o, k):
        g = at(o, k)
        return remote(qb.at[g], rb.at[g], ox_s.at[g], ox_r.at[g], a_dev[o])

    def os_(o, k):
        g = at(o, k)
        return remote(qs.at[g], rs.at[g], os_s.at[g], os_r.at[g], a_dev[o])

    def out_own(o, k):
        g = at(o, k)
        return pltpu.make_async_copy(
            ob.at[0, g], out.at[:, cols(o, side[o], k)], ol_sem.at[0, g])

    def out_got(o, k):
        g = at(o, k)
        return pltpu.make_async_copy(
            ob.at[1, g], out.at[:, cols(o, 1 - side[o], k)], ol_sem.at[1, g])

    def each(f):
        def body(k, carry):
            for o in orients:
                f(o, k)
            return carry
        lax.fori_loop(0, nc, body, 0)

    own = pltpu.make_async_copy(tok_in, tokb.at[core, z, 0], tl_sem)
    own.start()
    first = [remote(tok_in, tokb.at[core, z, 1 + i], ta_s.at[i], ta_r.at[i], a_dev[o])
             for i, o in enumerate(orients)]
    for c in first:
        c.start()

    def start_weights(o, k):
        px(o, k).start()
        py(o, k).start()
        wl(o, k).start()
    each(start_weights)

    own.wait()
    for c in first:
        c.wait()
    pair = pl.ds(z_hi * 2, 2)
    steps = (
        remote(tokb.at[core, z], tokb.at[core, z], tb_s.at[0], tb_r.at[0], z1_dev),
        remote(tokb.at[core, pair], tokb.at[core, pair], tb_s.at[1], tb_r.at[1], z2_dev),
        remote(tokb.at[core], tokb.at[core], tb_s.at[2], tb_r.at[2], c_dev),
    )
    for c in steps:
        c.start()
        c.wait()

    order = (row, y * 2 + (1 - x), (1 - y) * 2 + x, (1 - y) * 2 + (1 - x))
    for j in range(4):
        slot = owner[order[j]]
        for s in range(1 + len(orients)):
            lo = tokb[0, slot, s]
            hi = tokb[1, slot, s]
            al[s, :, j * panel:(j + 1) * panel] = jnp.concatenate([lo, hi], axis=1)

    kept = lax.broadcasted_iota(jnp.int32, (rows, cw), 0) < counts[0]

    def forward(o, k):
        px(o, k).wait_recv()
        fy(o, k).start()

    ahead = 2
    for k in range(ahead):
        for o in orients:
            forward(o, k)

    def compute(o, k):
        g = at(o, k)

        @pl.when(k + ahead < nc)
        def _():
            forward(o, k + ahead)

        wl(o, k).wait()
        py(o, k).wait_recv()
        fy(o, k).wait_recv()
        w = wb[g].reshape(4 * panel, cw)
        theirs = jnp.dot(al[1 + orients.index(o)], w, preferred_element_type=jnp.float32)
        split = theirs.reshape(GROUPS, rows // GROUPS, cw)
        top = jnp.maximum(jnp.max(jnp.abs(split), axis=1), 1.2e-38)
        inverse = 1.0 / top
        levels = jnp.round((split * inverse[:, None, :]) * 32767.0)
        qb[g] = levels.astype(jnp.int32).astype(jnp.int16).reshape(rows, cw)
        qs[g] = top
        ox(o, k).start()
        os_(o, k).start()
        mine = jnp.dot(al[0], w, preferred_element_type=jnp.float32)
        ob[0, g] = jnp.where(kept, mine, 0.0)
        out_own(o, k).start()
    each(compute)

    def receive(o, k):
        g = at(o, k)
        ox(o, k).wait_recv()
        os_(o, k).wait_recv()
        levels = rb[g].astype(jnp.int32).astype(jnp.float32).reshape(GROUPS, rows // GROUPS, cw)
        value = levels * (rs[g] * (1.0 / 32767.0))[:, None, :]
        ob[1, g] = jnp.where(kept, value.reshape(rows, cw), 0.0)
        out_got(o, k).start()
    each(receive)

    def finish(o, k):
        for c in (px(o, k), py(o, k), fy(o, k), ox(o, k), os_(o, k)):
            c.wait_send()
        out_own(o, k).wait()
        out_got(o, k).wait()
    each(finish)


def per_device(tokens, weight, counts, owner):
    rows, piece = tokens.shape
    panel, width = weight.shape
    orients = (0, 1)
    cw = 256
    nc = width // (2 * len(orients) * cw)
    nct = nc * len(orients)
    sets = 1 + len(orients)
    dma = pltpu.SemaphoreType.DMA
    return pl.pallas_call(
        functools.partial(kernel, orients, nc, cw),
        out_shape=jax.ShapeDtypeStruct((rows, width), jnp.float32),
        in_specs=[pl.BlockSpec(memory_space=pltpu.SMEM)] * 2 + [pl.BlockSpec(memory_space=pl.ANY)] * 2,
        out_specs=pl.BlockSpec(memory_space=pl.ANY),
        scratch_shapes=[
            pltpu.VMEM((2, 4, sets, rows, piece), jnp.bfloat16),
            pltpu.VMEM((sets, rows, 4 * panel), jnp.bfloat16),
            pltpu.VMEM((nct, 4, panel, cw), jnp.bfloat16),
            pltpu.VMEM((nct, rows, cw), jnp.int16),
            pltpu.VMEM((nct, GROUPS, cw), jnp.float32),
            pltpu.VMEM((nct, rows, cw), jnp.int16),
            pltpu.VMEM((nct, GROUPS, cw), jnp.float32),
            pltpu.VMEM((2, nct, rows, cw), jnp.float32),
            dma, dma((len(orients),)), dma((len(orients),)), dma((3,)), dma((3,)),
        ] + [dma((nct,))] * 11 + [dma((2, nct))],
        compiler_params=pltpu.CompilerParams(
            collective_id=0, has_side_effects=True, vmem_limit_bytes=56 * 2**20),
        cost_estimate=pl.CostEstimate(
            flops=2 * rows * 4 * panel * width, bytes_accessed=8 * rows * width, transcendentals=0),
    )(counts, owner, tokens, weight)


def solution(mesh):
    in_specs = (P("row", "col"), P("row", "col"), P("row"), P())
    out_specs = P("row", "col")
    planned = dict(mesh.shape) == {"row": 4, "col": 8}
    return jax.shard_map(
        per_device if planned else per_device_general,
        mesh=mesh, in_specs=in_specs, out_specs=out_specs, check_vma=False,
    )
```

```python
import functools

import jax
import jax.numpy as jnp
from jax import lax
from jax.experimental import pallas as pl
from jax.experimental.pallas import tpu as pltpu
from jax.sharding import PartitionSpec as P

MESH = pl.DeviceIdType.MESH
GROUPS = 8


def align_panels(gathered, owner):
    row_count = gathered.shape[0]
    panels = owner.shape[0]
    slotted = gathered.reshape(row_count, panels, gathered.shape[1] // panels)
    return jnp.take(slotted, owner, axis=1).reshape(row_count, gathered.shape[1])


def per_device_general(tokens, weight, counts, owner):
    row_count = tokens.shape[0]
    aligned = align_panels(lax.all_gather(tokens, "col", axis=1, tiled=True), owner)
    gathered_w = lax.all_gather(weight, "row", axis=0, tiled=True)
    product = jnp.dot(aligned, gathered_w, preferred_element_type=jnp.float32)
    token_limit = counts[0]
    kept = jnp.arange(row_count, dtype=jnp.int32) < token_limit
    return jnp.where(kept[:, None], product, jnp.float32(0.0))


def kernel(
    orients, nc, cw,
    counts, owner, tok_in, w_in, out,
    piece_buf, tokb, al, wb, qb, qs, rb, rs, ob,
    tl_sem, tc_s, tc_r, ta_s, ta_r, zr_s, zr_r, zl_s, zl_r, tm_s, tm_r,
    wl_sem, px_s, px_r, py_s, py_r, fy_s, fy_r, ox_s, ox_r, os_s, os_r, ol_sem,
):
    rows, piece = tok_in.shape
    panel = w_in.shape[0]
    half = nc * cw
    row, col = lax.axis_index("row"), lax.axis_index("col")
    y, x = row // 2, row % 2
    z, core = col // 2, col % 2
    part = rows // 2
    x_dev = (y * 2 + (1 - x), col)
    y_dev = ((1 - y) * 2 + x, col)
    up_dev = (row, lax.rem(z + 1, 4) * 2 + core)
    down_dev = (row, lax.rem(z + 3, 4) * 2 + core)
    c_dev = (row, z * 2 + (1 - core))
    peers = (x_dev, y_dev, up_dev, down_dev, c_dev)

    barrier = pltpu.get_barrier_semaphore()
    for peer in peers:
        pl.semaphore_signal(barrier, inc=1, device_id=peer, device_id_type=MESH)
    pl.semaphore_wait(barrier, len(peers))

    def remote(src, dst, send, recv, dev):
        return pltpu.make_async_remote_copy(
            src_ref=src, dst_ref=dst, send_sem=send, recv_sem=recv,
            device_id=dev, device_id_type=MESH)

    a_dev = (x_dev, y_dev)
    b_dev = (y_dev, x_dev)
    side = (x, y)

    def cols(o, s, k):
        return pl.ds(pl.multiple_of(orients.index(o) * 2 * half + s * half + k * cw, 128), cw)

    def at(o, k):
        return orients.index(o) * nc + k

    def px(o, k):
        g = at(o, k)
        return remote(w_in.at[:, cols(o, 1 - side[o], k)], wb.at[g, 1 + o],
                      px_s.at[g], px_r.at[g], a_dev[o])

    def py(o, k):
        g = at(o, k)
        return remote(w_in.at[:, cols(o, side[o], k)], wb.at[g, 2 - o],
                      py_s.at[g], py_r.at[g], b_dev[o])

    def fy(o, k):
        g = at(o, k)
        return remote(wb.at[g, 1 + o], wb.at[g, 3], fy_s.at[g], fy_r.at[g], b_dev[o])

    def wl(o, k):
        g = at(o, k)
        return pltpu.make_async_copy(
            w_in.at[:, cols(o, side[o], k)], wb.at[g, 0], wl_sem.at[g])

    def ox(o, k):
        g = at(o, k)
        return remote(qb.at[g], rb.at[g], ox_s.at[g], ox_r.at[g], a_dev[o])

    def os_(o, k):
        g = at(o, k)
        return remote(qs.at[g], rs.at[g], os_s.at[g], os_r.at[g], a_dev[o])

    def out_own(o, k):
        g = at(o, k)
        return pltpu.make_async_copy(
            ob.at[0, g], out.at[:, cols(o, side[o], k)], ol_sem.at[0, g])

    def out_got(o, k):
        g = at(o, k)
        return pltpu.make_async_copy(
            ob.at[1, g], out.at[:, cols(o, 1 - side[o], k)], ol_sem.at[1, g])

    def each(f):
        def body(k, carry):
            for o in orients:
                f(o, k)
            return carry
        lax.fori_loop(0, nc, body, 0)

    def start_weights(k):
        for o in orients:
            px(o, k).start()
            py(o, k).start()

    def rows_of(c):
        return pl.ds(pl.multiple_of(c * part, 16), part)

    own = pltpu.make_async_copy(tok_in.at[rows_of(core)], piece_buf.at[0], tl_sem)
    own.start()
    other = remote(tok_in.at[rows_of(1 - core)], piece_buf.at[1], tc_s, tc_r, c_dev)
    other.start()
    start_weights(0)
    own.wait()
    other.wait()
    mine_t, other_t = piece_buf[0], piece_buf[1]

    @pl.when(core == 0)
    def _():
        tokb[0, z, 0] = jnp.concatenate([mine_t, other_t], axis=1)

    @pl.when(core == 1)
    def _():
        tokb[1, z, 0] = jnp.concatenate([other_t, mine_t], axis=1)

    first = [remote(tokb.at[core, z, 0], tokb.at[core, z, 1 + i], ta_s.at[i], ta_r.at[i], a_dev[o])
             for i, o in enumerate(orients)]
    for c in first:
        c.start()
    start_weights(1)
    for c in first:
        c.wait_recv()

    def slot_copy(at_z, send, recv, dev):
        return remote(tokb.at[core, at_z], tokb.at[core, at_z], send, recv, dev)

    def mate(at_z):
        return slot_copy(at_z, tm_s.at[at_z], tm_r.at[at_z], c_dev)

    def up(s, shard):
        return slot_copy(shard, zr_s.at[s], zr_r.at[s], up_dev)

    def down(s, shard):
        return slot_copy(shard, zl_s.at[s], zl_r.at[s], down_dev)

    def send_step(s):
        @pl.when(jnp.logical_and(z < 3, z >= s))
        def _():
            up(s, z - s).start()

        @pl.when(jnp.logical_and(z > 0, z + s <= 3))
        def _():
            down(s, z + s).start()

    def recv_step(s):
        @pl.when(z >= s + 1)
        def _():
            up(s, z - 1 - s).wait_recv()
            mate(z - 1 - s).start()

        @pl.when(z + 1 + s <= 3)
        def _():
            down(s, z + 1 + s).wait_recv()
            mate(z + 1 + s).start()

    send_step(0)
    mate(z).start()

    def start_rest(k, carry):
        start_weights(k)
        return carry
    lax.fori_loop(2, nc, start_rest, 0)

    def start_own(o, k):
        wl(o, k).start()
    each(start_own)

    def forward(o, k):
        px(o, k).wait_recv()
        fy(o, k).start()

    ahead = 3
    for s in range(3):
        recv_step(s)
        if s < 2:
            send_step(s + 1)
        for o in orients:
            forward(o, s)
    for s in range(3):
        @pl.when(jnp.logical_and(z < 3, z >= s))
        def _():
            up(s, z - s).wait_send()

        @pl.when(jnp.logical_and(z > 0, z + s <= 3))
        def _():
            down(s, z + s).wait_send()
    for at_z in range(4):
        mate(at_z).wait_recv()
        mate(at_z).wait_send()
    for c in first:
        c.wait_send()

    order = (row, y * 2 + (1 - x), (1 - y) * 2 + x, (1 - y) * 2 + (1 - x))
    for j in range(4):
        slot = owner[order[j]]
        for s in range(1 + len(orients)):
            for c in range(2):
                al[s, c * part:(c + 1) * part, j * panel:(j + 1) * panel] = tokb[c, slot, s]

    kept = lax.broadcasted_iota(jnp.int32, (rows, cw), 0) < counts[0]

    def compute(o, k):
        g = at(o, k)

        @pl.when(k + ahead < nc)
        def _():
            forward(o, k + ahead)

        wl(o, k).wait()
        py(o, k).wait_recv()
        fy(o, k).wait_recv()
        w = wb[g].reshape(4 * panel, cw)
        theirs = jnp.dot(al[1 + orients.index(o)], w, preferred_element_type=jnp.float32)
        split = theirs.reshape(GROUPS, rows // GROUPS, cw)
        top = jnp.maximum(jnp.max(jnp.abs(split), axis=1), 1.2e-38)
        inverse = 1.0 / top
        levels = jnp.round((split * inverse[:, None, :]) * 32767.0)
        qb[g] = levels.astype(jnp.int32).astype(jnp.int16).reshape(rows, cw)
        qs[g] = top
        ox(o, k).start()
        os_(o, k).start()
        mine = jnp.dot(al[0], w, preferred_element_type=jnp.float32)
        ob[0, g] = jnp.where(kept, mine, 0.0)
        out_own(o, k).start()
    each(compute)

    def receive(o, k):
        g = at(o, k)
        ox(o, k).wait_recv()
        os_(o, k).wait_recv()
        levels = rb[g].astype(jnp.int32).astype(jnp.float32).reshape(GROUPS, rows // GROUPS, cw)
        value = levels * (rs[g] * (1.0 / 32767.0))[:, None, :]
        ob[1, g] = jnp.where(kept, value.reshape(rows, cw), 0.0)
        out_got(o, k).start()
    each(receive)

    def finish(o, k):
        for c in (px(o, k), py(o, k), fy(o, k), ox(o, k), os_(o, k)):
            c.wait_send()
        out_own(o, k).wait()
        out_got(o, k).wait()
    each(finish)


def per_device(tokens, weight, counts, owner):
    rows, piece = tokens.shape
    panel, width = weight.shape
    orients = (0, 1)
    cw = 256
    nc = width // (2 * len(orients) * cw)
    nct = nc * len(orients)
    sets = 1 + len(orients)
    dma = pltpu.SemaphoreType.DMA
    return pl.pallas_call(
        functools.partial(kernel, orients, nc, cw),
        out_shape=jax.ShapeDtypeStruct((rows, width), jnp.float32),
        in_specs=[pl.BlockSpec(memory_space=pltpu.SMEM)] * 2 + [pl.BlockSpec(memory_space=pl.ANY)] * 2,
        out_specs=pl.BlockSpec(memory_space=pl.ANY),
        scratch_shapes=[
            pltpu.VMEM((2, rows // 2, piece), jnp.bfloat16),
            pltpu.VMEM((2, 4, sets, rows // 2, panel), jnp.bfloat16),
            pltpu.VMEM((sets, rows, 4 * panel), jnp.bfloat16),
            pltpu.VMEM((nct, 4, panel, cw), jnp.bfloat16),
            pltpu.VMEM((nct, rows, cw), jnp.int16),
            pltpu.VMEM((nct, GROUPS, cw), jnp.float32),
            pltpu.VMEM((nct, rows, cw), jnp.int16),
            pltpu.VMEM((nct, GROUPS, cw), jnp.float32),
            pltpu.VMEM((2, nct, rows, cw), jnp.float32),
            dma, dma, dma, dma((len(orients),)), dma((len(orients),)),
            dma((3,)), dma((3,)), dma((3,)), dma((3,)), dma((4,)), dma((4,)),
        ] + [dma((nct,))] * 11 + [dma((2, nct))],
        compiler_params=pltpu.CompilerParams(
            collective_id=0, has_side_effects=True, vmem_limit_bytes=56 * 2**20),
        cost_estimate=pl.CostEstimate(
            flops=2 * rows * 4 * panel * width, bytes_accessed=8 * rows * width, transcendentals=0),
    )(counts, owner, tokens, weight)


def solution(mesh):
    in_specs = (P("row", "col"), P("row", "col"), P("row"), P())
    out_specs = P("row", "col")
    planned = dict(mesh.shape) == {"row": 4, "col": 8}
    return jax.shard_map(
        per_device if planned else per_device_general,
        mesh=mesh, in_specs=in_specs, out_specs=out_specs, check_vma=False,
    )
```

```python
import functools

import jax
import jax.numpy as jnp
from jax import lax
from jax.experimental import pallas as pl
from jax.experimental.pallas import tpu as pltpu
from jax.sharding import PartitionSpec as P

MESH = pl.DeviceIdType.MESH
GROUPS = 8


def align_panels(gathered, owner):
    row_count = gathered.shape[0]
    panels = owner.shape[0]
    slotted = gathered.reshape(row_count, panels, gathered.shape[1] // panels)
    return jnp.take(slotted, owner, axis=1).reshape(row_count, gathered.shape[1])


def per_device_general(tokens, weight, counts, owner):
    row_count = tokens.shape[0]
    aligned = align_panels(lax.all_gather(tokens, "col", axis=1, tiled=True), owner)
    gathered_w = lax.all_gather(weight, "row", axis=0, tiled=True)
    product = jnp.dot(aligned, gathered_w, preferred_element_type=jnp.float32)
    token_limit = counts[0]
    kept = jnp.arange(row_count, dtype=jnp.int32) < token_limit
    return jnp.where(kept[:, None], product, jnp.float32(0.0))


def kernel(
    orients, nc, cw,
    counts, owner, tok_in, w_in, ob,
    piece_buf, tokb, al, wb, qb, qs, rb, rs,
    tl_sem, tc_s, tc_r, ta_s, ta_r, zr_s, zr_r, zl_s, zl_r, tm_s, tm_r,
    wl_sem, px_s, px_r, py_s, py_r, fy_s, fy_r, ox_s, ox_r, os_s, os_r,
):
    piece, rows = tok_in.shape
    panel = w_in.shape[0]
    half = nc * cw
    row, col = lax.axis_index("row"), lax.axis_index("col")
    y, x = row // 2, row % 2
    z, core = col // 2, col % 2
    part = rows // 2
    x_dev = (y * 2 + (1 - x), col)
    y_dev = ((1 - y) * 2 + x, col)
    up_dev = (row, lax.rem(z + 1, 4) * 2 + core)
    down_dev = (row, lax.rem(z + 3, 4) * 2 + core)
    c_dev = (row, z * 2 + (1 - core))
    peers = (x_dev, y_dev, up_dev, down_dev, c_dev)

    barrier = pltpu.get_barrier_semaphore()
    for peer in peers:
        pl.semaphore_signal(barrier, inc=1, device_id=peer, device_id_type=MESH)
    pl.semaphore_wait(barrier, len(peers))

    def remote(src, dst, send, recv, dev):
        return pltpu.make_async_remote_copy(
            src_ref=src, dst_ref=dst, send_sem=send, recv_sem=recv,
            device_id=dev, device_id_type=MESH)

    a_dev = (x_dev, y_dev)
    b_dev = (y_dev, x_dev)
    side = (x, y)

    def cols(o, s, k):
        return pl.ds(pl.multiple_of(orients.index(o) * 2 * half + s * half + k * cw, 128), cw)

    def at(o, k):
        return orients.index(o) * nc + k

    def px(o, k):
        g = at(o, k)
        return remote(w_in.at[:, cols(o, 1 - side[o], k)], wb.at[g, 1 + o],
                      px_s.at[g], px_r.at[g], a_dev[o])

    def py(o, k):
        g = at(o, k)
        return remote(w_in.at[:, cols(o, side[o], k)], wb.at[g, 2 - o],
                      py_s.at[g], py_r.at[g], b_dev[o])

    def fy(o, k):
        g = at(o, k)
        return remote(wb.at[g, 1 + o], wb.at[g, 3], fy_s.at[g], fy_r.at[g], b_dev[o])

    def wl(o, k):
        g = at(o, k)
        return pltpu.make_async_copy(
            w_in.at[:, cols(o, side[o], k)], wb.at[g, 0], wl_sem.at[g])

    def ox(o, k):
        g = at(o, k)
        return remote(qb.at[g], rb.at[g], ox_s.at[g], ox_r.at[g], a_dev[o])

    def os_(o, k):
        g = at(o, k)
        return remote(qs.at[g], rs.at[g], os_s.at[g], os_r.at[g], a_dev[o])

    def each(f):
        def body(k, carry):
            for o in orients:
                f(o, k)
            return carry
        lax.fori_loop(0, nc, body, 0)

    def start_weights(k):
        for o in orients:
            px(o, k).start()
            py(o, k).start()

    def rows_of(c):
        return pl.ds(pl.multiple_of(c * part, 128), part)

    own = pltpu.make_async_copy(tok_in.at[:, rows_of(core)], piece_buf.at[0], tl_sem)
    own.start()
    other = remote(tok_in.at[:, rows_of(1 - core)], piece_buf.at[1], tc_s, tc_r, c_dev)
    other.start()
    start_weights(0)
    own.wait()
    other.wait()
    mine_t, other_t = piece_buf[0], piece_buf[1]

    @pl.when(core == 0)
    def _():
        tokb[0, z, 0] = jnp.concatenate([mine_t, other_t], axis=0).T

    @pl.when(core == 1)
    def _():
        tokb[1, z, 0] = jnp.concatenate([other_t, mine_t], axis=0).T

    first = [remote(tokb.at[core, z, 0], tokb.at[core, z, 1 + i], ta_s.at[i], ta_r.at[i], a_dev[o])
             for i, o in enumerate(orients)]
    for c in first:
        c.start()
    start_weights(1)
    for c in first:
        c.wait_recv()

    def slot_copy(at_z, send, recv, dev):
        return remote(tokb.at[core, at_z], tokb.at[core, at_z], send, recv, dev)

    def mate(at_z):
        return slot_copy(at_z, tm_s.at[at_z], tm_r.at[at_z], c_dev)

    def up(s, shard):
        return slot_copy(shard, zr_s.at[s], zr_r.at[s], up_dev)

    def down(s, shard):
        return slot_copy(shard, zl_s.at[s], zl_r.at[s], down_dev)

    def send_step(s):
        @pl.when(jnp.logical_and(z < 3, z >= s))
        def _():
            up(s, z - s).start()

        @pl.when(jnp.logical_and(z > 0, z + s <= 3))
        def _():
            down(s, z + s).start()

    def recv_step(s):
        @pl.when(z >= s + 1)
        def _():
            up(s, z - 1 - s).wait_recv()
            mate(z - 1 - s).start()

        @pl.when(z + 1 + s <= 3)
        def _():
            down(s, z + 1 + s).wait_recv()
            mate(z + 1 + s).start()

    send_step(0)
    mate(z).start()

    def start_rest(k, carry):
        start_weights(k)
        return carry
    lax.fori_loop(2, nc, start_rest, 0)

    def start_own(o, k):
        wl(o, k).start()
    each(start_own)

    def forward(o, k):
        px(o, k).wait_recv()
        fy(o, k).start()

    ahead = 3
    for s in range(3):
        recv_step(s)
        if s < 2:
            send_step(s + 1)
        for o in orients:
            forward(o, s)
    for s in range(3):
        @pl.when(jnp.logical_and(z < 3, z >= s))
        def _():
            up(s, z - s).wait_send()

        @pl.when(jnp.logical_and(z > 0, z + s <= 3))
        def _():
            down(s, z + s).wait_send()
    for at_z in range(4):
        mate(at_z).wait_recv()
        mate(at_z).wait_send()
    for c in first:
        c.wait_send()

    order = (row, y * 2 + (1 - x), (1 - y) * 2 + x, (1 - y) * 2 + (1 - x))
    for j in range(4):
        slot = owner[order[j]]
        for s in range(1 + len(orients)):
            for c in range(2):
                al[s, c * part:(c + 1) * part, j * panel:(j + 1) * panel] = tokb[c, slot, s]

    kept = lax.broadcasted_iota(jnp.int32, (rows, cw), 0) < counts[0]

    def compute(o, k):
        g = at(o, k)

        @pl.when(k + ahead < nc)
        def _():
            forward(o, k + ahead)

        wl(o, k).wait()
        py(o, k).wait_recv()
        fy(o, k).wait_recv()
        w = wb[g].reshape(4 * panel, cw)
        theirs = jnp.dot(al[1 + orients.index(o)], w, preferred_element_type=jnp.float32)
        split = theirs.reshape(GROUPS, rows // GROUPS, cw)
        top = jnp.maximum(jnp.max(jnp.abs(split), axis=1), 1.2e-38)
        inverse = 1.0 / top
        levels = jnp.round((split * inverse[:, None, :]) * 32767.0)
        qb[g] = levels.astype(jnp.int32).astype(jnp.int16).reshape(rows, cw)
        qs[g] = top
        ox(o, k).start()
        os_(o, k).start()
        mine = jnp.dot(al[0], w, preferred_element_type=jnp.float32)
        ob[0, g] = jnp.where(kept, mine, 0.0)
    each(compute)

    def receive(o, k):
        g = at(o, k)
        ox(o, k).wait_recv()
        os_(o, k).wait_recv()
        levels = rb[g].astype(jnp.int32).astype(jnp.float32).reshape(GROUPS, rows // GROUPS, cw)
        value = levels * (rs[g] * (1.0 / 32767.0))[:, None, :]
        ob[1, g] = jnp.where(kept, value.reshape(rows, cw), 0.0)
    each(receive)

    def finish(o, k):
        for c in (px(o, k), py(o, k), fy(o, k), ox(o, k), os_(o, k)):
            c.wait_send()
    each(finish)


def store_kernel(orients, nc, cw, ob, out, sem):
    row = lax.axis_index("row")
    side = (row % 2, row // 2)

    def each(act):
        def body(k, carry):
            for i, o in enumerate(orients):
                for got in range(2):
                    s = 1 - side[o] if got else side[o]
                    start = pl.multiple_of((i * 2 + s) * nc * cw + k * cw, 128)
                    copy = pltpu.make_async_copy(
                        ob.at[got, i * nc + k], out.at[:, pl.ds(start, cw)], sem.at[got, i * nc + k])
                    act(copy)
            return carry
        lax.fori_loop(0, nc, body, 0)
    each(lambda copy: copy.start())
    each(lambda copy: copy.wait())


def per_device(tokens, weight, counts, owner):
    rows, piece = tokens.shape
    panel, width = weight.shape
    orients = (0, 1)
    cw = 256
    nc = width // (2 * len(orients) * cw)
    nct = nc * len(orients)
    sets = 1 + len(orients)
    dma = pltpu.SemaphoreType.DMA
    blocks = pl.pallas_call(
        functools.partial(kernel, orients, nc, cw),
        out_shape=pltpu.VMEM((2, nct, rows, cw), jnp.float32),
        in_specs=[pl.BlockSpec(memory_space=pltpu.SMEM)] * 2 + [pl.BlockSpec(memory_space=pl.ANY)] * 2,
        out_specs=pl.BlockSpec(memory_space=pltpu.VMEM),
        scratch_shapes=[
            pltpu.VMEM((2, piece, rows // 2), jnp.bfloat16),
            pltpu.VMEM((2, 4, sets, rows // 2, panel), jnp.bfloat16),
            pltpu.VMEM((sets, rows, 4 * panel), jnp.bfloat16),
            pltpu.VMEM((nct, 4, panel, cw), jnp.bfloat16),
            pltpu.VMEM((nct, rows, cw), jnp.int16),
            pltpu.VMEM((nct, GROUPS, cw), jnp.float32),
            pltpu.VMEM((nct, rows, cw), jnp.int16),
            pltpu.VMEM((nct, GROUPS, cw), jnp.float32),
            dma, dma, dma, dma((len(orients),)), dma((len(orients),)),
            dma((3,)), dma((3,)), dma((3,)), dma((3,)), dma((4,)), dma((4,)),
        ] + [dma((nct,))] * 11,
        compiler_params=pltpu.CompilerParams(
            collective_id=0, has_side_effects=True, vmem_limit_bytes=48 * 2**20),
        cost_estimate=pl.CostEstimate(
            flops=2 * rows * 4 * panel * width, bytes_accessed=8 * rows * width, transcendentals=0),
    )(counts, owner, tokens.T, weight)
    return pl.pallas_call(
        functools.partial(store_kernel, orients, nc, cw),
        out_shape=jax.ShapeDtypeStruct((rows, width), jnp.float32),
        in_specs=[pl.BlockSpec(memory_space=pltpu.VMEM)],
        out_specs=pl.BlockSpec(memory_space=pl.ANY),
        scratch_shapes=[dma((2, nct))],
        compiler_params=pltpu.CompilerParams(vmem_limit_bytes=16 * 2**20),
    )(pltpu.with_memory_space_constraint(blocks, pltpu.VMEM))


def solution(mesh):
    in_specs = (P("row", "col"), P("row", "col"), P("row"), P())
    out_specs = P("row", "col")
    planned = dict(mesh.shape) == {"row": 4, "col": 8}
    return jax.shard_map(
        per_device if planned else per_device_general,
        mesh=mesh, in_specs=in_specs, out_specs=out_specs, check_vma=False,
    )
```

```python
import functools

import jax
import jax.numpy as jnp
from jax import lax
from jax.experimental import pallas as pl
from jax.experimental.pallas import tpu as pltpu
from jax.sharding import PartitionSpec as P

MESH = pl.DeviceIdType.MESH
GROUPS = 2


def align_panels(gathered, owner):
    row_count = gathered.shape[0]
    panels = owner.shape[0]
    slotted = gathered.reshape(row_count, panels, gathered.shape[1] // panels)
    return jnp.take(slotted, owner, axis=1).reshape(row_count, gathered.shape[1])


def per_device_general(tokens, weight, counts, owner):
    row_count = tokens.shape[0]
    aligned = align_panels(lax.all_gather(tokens, "col", axis=1, tiled=True), owner)
    gathered_w = lax.all_gather(weight, "row", axis=0, tiled=True)
    product = jnp.dot(aligned, gathered_w, preferred_element_type=jnp.float32)
    token_limit = counts[0]
    kept = jnp.arange(row_count, dtype=jnp.int32) < token_limit
    return jnp.where(kept[:, None], product, jnp.float32(0.0))


def kernel(
    orients, nc, cw,
    counts, owner, tok_in, w_in, ob,
    piece_buf, tokb, al, wb, qb, qs, rb, rs,
    tl_sem, tc_s, tc_r, ta_s, ta_r, zr_s, zr_r, zl_s, zl_r, tm_s, tm_r,
    wl_sem, px_s, px_r, py_s, py_r, fy_s, fy_r, ox_s, ox_r, os_s, os_r,
):
    piece, rows = tok_in.shape
    panel = w_in.shape[0]
    half = nc * cw
    row, col = lax.axis_index("row"), lax.axis_index("col")
    y, x = row // 2, row % 2
    z, core = col // 2, col % 2
    part = rows // 2
    x_dev = (y * 2 + (1 - x), col)
    y_dev = ((1 - y) * 2 + x, col)
    up_dev = (row, lax.rem(z + 1, 4) * 2 + core)
    down_dev = (row, lax.rem(z + 3, 4) * 2 + core)
    c_dev = (row, z * 2 + (1 - core))
    peers = (x_dev, y_dev, up_dev, down_dev, c_dev)

    barrier = pltpu.get_barrier_semaphore()
    for peer in peers:
        pl.semaphore_signal(barrier, inc=1, device_id=peer, device_id_type=MESH)
    pl.semaphore_wait(barrier, len(peers))

    def remote(src, dst, send, recv, dev):
        return pltpu.make_async_remote_copy(
            src_ref=src, dst_ref=dst, send_sem=send, recv_sem=recv,
            device_id=dev, device_id_type=MESH)

    a_dev = (x_dev, y_dev)
    b_dev = (y_dev, x_dev)
    side = (x, y)

    def cols(o, s, k):
        return pl.ds(pl.multiple_of(orients.index(o) * 2 * half + s * half + k * cw, 128), cw)

    def at(o, k):
        return orients.index(o) * nc + k

    def px(o, k):
        g = at(o, k)
        return remote(w_in.at[:, cols(o, 1 - side[o], k)], wb.at[g, 1 + o],
                      px_s.at[g], px_r.at[g], a_dev[o])

    def py(o, k):
        g = at(o, k)
        return remote(w_in.at[:, cols(o, side[o], k)], wb.at[g, 2 - o],
                      py_s.at[g], py_r.at[g], b_dev[o])

    def fy(o, k):
        g = at(o, k)
        return remote(wb.at[g, 1 + o], wb.at[g, 3], fy_s.at[g], fy_r.at[g], b_dev[o])

    def wl(o, k):
        g = at(o, k)
        return pltpu.make_async_copy(
            w_in.at[:, cols(o, side[o], k)], wb.at[g, 0], wl_sem.at[g])

    def ox(o, k):
        g = at(o, k)
        return remote(qb.at[g], rb.at[g], ox_s.at[g], ox_r.at[g], a_dev[o])

    def os_(o, k):
        g = at(o, k)
        return remote(qs.at[g], rs.at[g], os_s.at[g], os_r.at[g], a_dev[o])

    def each(f):
        def body(k, carry):
            for o in orients:
                f(o, k)
            return carry
        lax.fori_loop(0, nc, body, 0)

    def start_weights(k):
        for o in orients:
            px(o, k).start()
            py(o, k).start()

    def rows_of(c):
        return pl.ds(pl.multiple_of(c * part, 128), part)

    own = pltpu.make_async_copy(tok_in.at[:, rows_of(core)], piece_buf.at[0], tl_sem)
    own.start()
    other = remote(tok_in.at[:, rows_of(1 - core)], piece_buf.at[1], tc_s, tc_r, c_dev)
    other.start()
    start_weights(0)
    own.wait()
    other.wait()
    mine_t, other_t = piece_buf[0], piece_buf[1]

    @pl.when(core == 0)
    def _():
        tokb[0, z, 0] = jnp.concatenate([mine_t, other_t], axis=0).T

    @pl.when(core == 1)
    def _():
        tokb[1, z, 0] = jnp.concatenate([other_t, mine_t], axis=0).T

    first = [remote(tokb.at[core, z, 0], tokb.at[core, z, 1 + i], ta_s.at[i], ta_r.at[i], a_dev[o])
             for i, o in enumerate(orients)]
    for c in first:
        c.start()
    start_weights(1)
    for c in first:
        c.wait_recv()

    def slot_copy(at_z, send, recv, dev):
        return remote(tokb.at[core, at_z], tokb.at[core, at_z], send, recv, dev)

    def mate(at_z):
        return slot_copy(at_z, tm_s.at[at_z], tm_r.at[at_z], c_dev)

    def up(s, shard):
        return slot_copy(shard, zr_s.at[s], zr_r.at[s], up_dev)

    def down(s, shard):
        return slot_copy(shard, zl_s.at[s], zl_r.at[s], down_dev)

    def send_step(s):
        @pl.when(jnp.logical_and(z < 3, z >= s))
        def _():
            up(s, z - s).start()

        @pl.when(jnp.logical_and(z > 0, z + s <= 3))
        def _():
            down(s, z + s).start()

    def recv_step(s):
        @pl.when(z >= s + 1)
        def _():
            up(s, z - 1 - s).wait_recv()
            mate(z - 1 - s).start()

        @pl.when(z + 1 + s <= 3)
        def _():
            down(s, z + 1 + s).wait_recv()
            mate(z + 1 + s).start()

    send_step(0)
    mate(z).start()

    def start_rest(k, carry):
        start_weights(k)
        return carry
    lax.fori_loop(2, nc, start_rest, 0)

    def start_own(o, k):
        wl(o, k).start()
    each(start_own)

    def forward(o, k):
        px(o, k).wait_recv()
        fy(o, k).start()

    ahead = 3
    for s in range(3):
        recv_step(s)
        if s < 2:
            send_step(s + 1)
        for o in orients:
            forward(o, s)
    for s in range(3):
        @pl.when(jnp.logical_and(z < 3, z >= s))
        def _():
            up(s, z - s).wait_send()

        @pl.when(jnp.logical_and(z > 0, z + s <= 3))
        def _():
            down(s, z + s).wait_send()
    for at_z in range(4):
        mate(at_z).wait_recv()
        mate(at_z).wait_send()
    for c in first:
        c.wait_send()

    order = (row, y * 2 + (1 - x), (1 - y) * 2 + x, (1 - y) * 2 + (1 - x))
    for j in range(4):
        slot = owner[order[j]]
        for s in range(1 + len(orients)):
            for c in range(2):
                al[s, c * part:(c + 1) * part, j * panel:(j + 1) * panel] = tokb[c, slot, s]

    kept = lax.broadcasted_iota(jnp.int32, (rows, cw), 0) < counts[0]

    def compute(o, k):
        g = at(o, k)

        @pl.when(k + ahead < nc)
        def _():
            forward(o, k + ahead)

        wl(o, k).wait()
        py(o, k).wait_recv()
        fy(o, k).wait_recv()
        w = wb[g].reshape(4 * panel, cw)
        theirs = jnp.dot(al[1 + orients.index(o)], w, preferred_element_type=jnp.float32)
        split = theirs.reshape(GROUPS, rows // GROUPS, cw)
        top = jnp.maximum(jnp.max(jnp.abs(split), axis=1), 1.2e-38)
        inverse = 1.0 / top
        levels = jnp.round((split * inverse[:, None, :]) * 32767.0)
        qb[g] = levels.astype(jnp.int32).astype(jnp.int16).reshape(rows, cw)
        qs[g] = top
        ox(o, k).start()
        os_(o, k).start()
        mine = jnp.dot(al[0], w, preferred_element_type=jnp.float32)
        ob[:, cols(o, side[o], k)] = jnp.where(kept, mine, 0.0)
    each(compute)

    def sent(o, k):
        for c in (px(o, k), py(o, k), fy(o, k)):
            c.wait_send()
    each(sent)

    def receive(o, k):
        g = at(o, k)
        ox(o, k).wait()
        os_(o, k).wait()
        levels = rb[g].astype(jnp.int32).astype(jnp.float32).reshape(GROUPS, rows // GROUPS, cw)
        value = levels * (rs[g] * (1.0 / 32767.0))[:, None, :]
        ob[:, cols(o, 1 - side[o], k)] = jnp.where(kept, value.reshape(rows, cw), 0.0)
    each(receive)


def store_kernel(parts, ob, out, sem):
    step = ob.shape[0] // parts
    copies = [pltpu.make_async_copy(ob.at[pl.ds(i * step, step)], out.at[pl.ds(i * step, step)], sem.at[i])
              for i in range(parts)]
    for c in copies:
        c.start()
    for c in copies:
        c.wait()


def per_device(tokens, weight, counts, owner):
    rows, piece = tokens.shape
    panel, width = weight.shape
    orients = (0, 1)
    cw = 512
    parts = 8
    nc = width // (2 * len(orients) * cw)
    nct = nc * len(orients)
    sets = 1 + len(orients)
    dma = pltpu.SemaphoreType.DMA
    blocks = pl.pallas_call(
        functools.partial(kernel, orients, nc, cw),
        out_shape=pltpu.VMEM((rows, width), jnp.float32),
        in_specs=[pl.BlockSpec(memory_space=pltpu.SMEM)] * 2 + [pl.BlockSpec(memory_space=pl.ANY)] * 2,
        out_specs=pl.BlockSpec(memory_space=pltpu.VMEM),
        scratch_shapes=[
            pltpu.VMEM((2, piece, rows // 2), jnp.bfloat16),
            pltpu.VMEM((2, 4, sets, rows // 2, panel), jnp.bfloat16),
            pltpu.VMEM((sets, rows, 4 * panel), jnp.bfloat16),
            pltpu.VMEM((nct, 4, panel, cw), jnp.bfloat16),
            pltpu.VMEM((nct, rows, cw), jnp.int16),
            pltpu.VMEM((nct, GROUPS, cw), jnp.float32),
            pltpu.VMEM((nct, rows, cw), jnp.int16),
            pltpu.VMEM((nct, GROUPS, cw), jnp.float32),
            dma, dma, dma, dma((len(orients),)), dma((len(orients),)),
            dma((3,)), dma((3,)), dma((3,)), dma((3,)), dma((4,)), dma((4,)),
        ] + [dma((nct,))] * 11,
        compiler_params=pltpu.CompilerParams(
            collective_id=0, has_side_effects=True, vmem_limit_bytes=48 * 2**20),
        cost_estimate=pl.CostEstimate(
            flops=2 * rows * 4 * panel * width, bytes_accessed=8 * rows * width, transcendentals=0),
    )(counts, owner, tokens.T, weight)
    return pl.pallas_call(
        functools.partial(store_kernel, parts),
        out_shape=jax.ShapeDtypeStruct((rows, width), jnp.float32),
        in_specs=[pl.BlockSpec(memory_space=pltpu.VMEM)],
        out_specs=pl.BlockSpec(memory_space=pl.ANY),
        scratch_shapes=[dma((parts,))],
        compiler_params=pltpu.CompilerParams(vmem_limit_bytes=16 * 2**20),
    )(pltpu.with_memory_space_constraint(blocks, pltpu.VMEM))


def solution(mesh):
    in_specs = (P("row", "col"), P("row", "col"), P("row"), P())
    out_specs = P("row", "col")
    planned = dict(mesh.shape) == {"row": 4, "col": 8}
    return jax.shard_map(
        per_device if planned else per_device_general,
        mesh=mesh, in_specs=in_specs, out_specs=out_specs, check_vma=False,
    )
```

```python
import functools

import jax
import jax.numpy as jnp
from jax import lax
from jax.experimental import pallas as pl
from jax.experimental.pallas import tpu as pltpu
from jax.sharding import PartitionSpec as P

MESH = pl.DeviceIdType.MESH
GROUPS = 2


def align_panels(gathered, owner):
    row_count = gathered.shape[0]
    panels = owner.shape[0]
    slotted = gathered.reshape(row_count, panels, gathered.shape[1] // panels)
    return jnp.take(slotted, owner, axis=1).reshape(row_count, gathered.shape[1])


def per_device_general(tokens, weight, counts, owner):
    row_count = tokens.shape[0]
    aligned = align_panels(lax.all_gather(tokens, "col", axis=1, tiled=True), owner)
    gathered_w = lax.all_gather(weight, "row", axis=0, tiled=True)
    product = jnp.dot(aligned, gathered_w, preferred_element_type=jnp.float32)
    token_limit = counts[0]
    kept = jnp.arange(row_count, dtype=jnp.int32) < token_limit
    return jnp.where(kept[:, None], product, jnp.float32(0.0))


def kernel(
    orients, nc, cw,
    counts, owner, tok_in, w_in, ob,
    piece_buf, tokb, al, wb, qb, qs, rb, rs,
    tl_sem, tc_s, tc_r, ta_s, ta_r, zr_s, zr_r, zl_s, zl_r, tm_s, tm_r,
    wl_sem, px_s, px_r, py_s, py_r, fy_s, fy_r, ox_s, ox_r, os_s, os_r,
):
    piece, rows = tok_in.shape
    panel = w_in.shape[0]
    half = nc * cw
    row, col = lax.axis_index("row"), lax.axis_index("col")
    y, x = row // 2, row % 2
    z, core = col // 2, col % 2
    part = rows // 2
    x_dev = (y * 2 + (1 - x), col)
    y_dev = ((1 - y) * 2 + x, col)
    up_dev = (row, lax.rem(z + 1, 4) * 2 + core)
    down_dev = (row, lax.rem(z + 3, 4) * 2 + core)
    c_dev = (row, z * 2 + (1 - core))
    peers = (x_dev, y_dev, up_dev, down_dev, c_dev)

    barrier = pltpu.get_barrier_semaphore()
    for peer in peers:
        pl.semaphore_signal(barrier, inc=1, device_id=peer, device_id_type=MESH)
    pl.semaphore_wait(barrier, len(peers))

    def remote(src, dst, send, recv, dev):
        return pltpu.make_async_remote_copy(
            src_ref=src, dst_ref=dst, send_sem=send, recv_sem=recv,
            device_id=dev, device_id_type=MESH)

    a_dev = (x_dev, y_dev)
    b_dev = (y_dev, x_dev)
    side = (x, y)

    def cols(o, s, k):
        return pl.ds(pl.multiple_of(orients.index(o) * 2 * half + s * half + k * cw, 128), cw)

    def at(o, k):
        return orients.index(o) * nc + k

    def px(o, k):
        g = at(o, k)
        return remote(w_in.at[:, cols(o, 1 - side[o], k)], wb.at[g, 1 + o],
                      px_s.at[g], px_r.at[g], a_dev[o])

    def py(o, k):
        g = at(o, k)
        return remote(w_in.at[:, cols(o, side[o], k)], wb.at[g, 2 - o],
                      py_s.at[g], py_r.at[g], b_dev[o])

    def fy(o, k):
        g = at(o, k)
        return remote(wb.at[g, 1 + o], wb.at[g, 3], fy_s.at[g], fy_r.at[g], b_dev[o])

    def wl(o, k):
        g = at(o, k)
        return pltpu.make_async_copy(
            w_in.at[:, cols(o, side[o], k)], wb.at[g, 0], wl_sem.at[g])

    def ox(o, k):
        g = at(o, k)
        return remote(qb.at[g], rb.at[g], ox_s.at[g], ox_r.at[g], a_dev[o])

    def os_(o, k):
        g = at(o, k)
        return remote(qs.at[g], rs.at[g], os_s.at[g], os_r.at[g], a_dev[o])

    def each(f):
        def body(k, carry):
            for o in orients:
                f(o, k)
            return carry
        lax.fori_loop(0, nc, body, 0)

    def start_weights(k):
        for o in orients:
            px(o, k).start()
            py(o, k).start()

    def rows_of(c):
        return pl.ds(pl.multiple_of(c * part, 128), part)

    own = pltpu.make_async_copy(tok_in.at[:, rows_of(core)], piece_buf.at[0], tl_sem)
    own.start()
    other = remote(tok_in.at[:, rows_of(1 - core)], piece_buf.at[1], tc_s, tc_r, c_dev)
    other.start()
    start_weights(0)
    own.wait()
    other.wait()
    mine_t, other_t = piece_buf[0], piece_buf[1]

    @pl.when(core == 0)
    def _():
        tokb[0, z, 0] = jnp.concatenate([mine_t, other_t], axis=0).T

    @pl.when(core == 1)
    def _():
        tokb[1, z, 0] = jnp.concatenate([other_t, mine_t], axis=0).T

    first = [remote(tokb.at[core, z, 0], tokb.at[core, z, 1 + i], ta_s.at[i], ta_r.at[i], a_dev[o])
             for i, o in enumerate(orients)]
    for c in first:
        c.start()
    start_weights(1)
    for c in first:
        c.wait_recv()

    def slot_copy(at_z, send, recv, dev):
        return remote(tokb.at[core, at_z], tokb.at[core, at_z], send, recv, dev)

    def mate(at_z):
        return slot_copy(at_z, tm_s.at[at_z], tm_r.at[at_z], c_dev)

    def up(s, shard):
        return slot_copy(shard, zr_s.at[s], zr_r.at[s], up_dev)

    def down(s, shard):
        return slot_copy(shard, zl_s.at[s], zl_r.at[s], down_dev)

    def send_step(s):
        @pl.when(jnp.logical_and(z < 3, z >= s))
        def _():
            up(s, z - s).start()

        @pl.when(jnp.logical_and(z > 0, z + s <= 3))
        def _():
            down(s, z + s).start()

    def recv_step(s):
        @pl.when(z >= s + 1)
        def _():
            up(s, z - 1 - s).wait_recv()
            mate(z - 1 - s).start()

        @pl.when(z + 1 + s <= 3)
        def _():
            down(s, z + 1 + s).wait_recv()
            mate(z + 1 + s).start()

    send_step(0)
    mate(z).start()

    def start_rest(k, carry):
        start_weights(k)
        return carry
    lax.fori_loop(2, nc, start_rest, 0)

    def start_own(o, k):
        wl(o, k).start()
    each(start_own)

    def forward(o, k):
        px(o, k).wait_recv()
        fy(o, k).start()

    ahead = 3
    for s in range(3):
        recv_step(s)
        if s < 2:
            send_step(s + 1)
        for o in orients:
            forward(o, s)
    for s in range(3):
        @pl.when(jnp.logical_and(z < 3, z >= s))
        def _():
            up(s, z - s).wait_send()

        @pl.when(jnp.logical_and(z > 0, z + s <= 3))
        def _():
            down(s, z + s).wait_send()
    for at_z in range(4):
        mate(at_z).wait_recv()
        mate(at_z).wait_send()
    for c in first:
        c.wait_send()

    order = (row, y * 2 + (1 - x), (1 - y) * 2 + x, (1 - y) * 2 + (1 - x))
    for j in range(4):
        slot = owner[order[j]]
        for s in range(1 + len(orients)):
            for c in range(2):
                al[s, c * part:(c + 1) * part, j * panel:(j + 1) * panel] = tokb[c, slot, s]

    kept = lax.broadcasted_iota(jnp.int32, (rows, cw), 0) < counts[0]

    def compute(o, k):
        g = at(o, k)

        @pl.when(k + ahead < nc)
        def _():
            forward(o, k + ahead)

        wl(o, k).wait()
        py(o, k).wait_recv()
        fy(o, k).wait_recv()
        w = wb[g].reshape(4 * panel, cw)
        theirs = jnp.dot(al[1 + orients.index(o)], w, preferred_element_type=jnp.float32)
        split = theirs.reshape(GROUPS, rows // GROUPS, cw)
        top = jnp.maximum(jnp.max(jnp.abs(split), axis=1), 1.2e-38)
        inverse = 1.0 / top
        levels = jnp.round((split * inverse[:, None, :]) * 32767.0)
        qb[g] = levels.astype(jnp.int32).astype(jnp.int16).reshape(rows, cw)
        qs[g] = top
        ox(o, k).start()
        os_(o, k).start()
        mine = jnp.dot(al[0], w, preferred_element_type=jnp.float32)
        ob[:, cols(o, side[o], k)] = jnp.where(kept, mine, 0.0)
    each(compute)

    def sent(o, k):
        for c in (px(o, k), py(o, k), fy(o, k)):
            c.wait_send()
    each(sent)

    def receive(o, k):
        g = at(o, k)
        ox(o, k).wait()
        os_(o, k).wait()
        levels = rb[g].astype(jnp.int32).astype(jnp.float32).reshape(GROUPS, rows // GROUPS, cw)
        value = levels * (rs[g] * (1.0 / 32767.0))[:, None, :]
        ob[:, cols(o, 1 - side[o], k)] = jnp.where(kept, value.reshape(rows, cw), 0.0)
    each(receive)


def store_kernel(parts, ob, out, sem):
    step = ob.shape[0] // parts
    copies = [pltpu.make_async_copy(ob.at[pl.ds(i * step, step)], out.at[pl.ds(i * step, step)], sem.at[i])
              for i in range(parts)]
    for c in copies:
        c.start()
    for c in copies:
        c.wait()


def per_device(tokens, weight, counts, owner):
    rows, piece = tokens.shape
    panel, width = weight.shape
    orients = (0, 1)
    cw = 384
    parts = 8
    nc = width // (2 * len(orients) * cw)
    nct = nc * len(orients)
    sets = 1 + len(orients)
    dma = pltpu.SemaphoreType.DMA
    blocks = pl.pallas_call(
        functools.partial(kernel, orients, nc, cw),
        out_shape=pltpu.VMEM((rows, width), jnp.float32),
        in_specs=[pl.BlockSpec(memory_space=pltpu.SMEM)] * 2 + [pl.BlockSpec(memory_space=pl.ANY)] * 2,
        out_specs=pl.BlockSpec(memory_space=pltpu.VMEM),
        scratch_shapes=[
            pltpu.VMEM((2, piece, rows // 2), jnp.bfloat16),
            pltpu.VMEM((2, 4, sets, rows // 2, panel), jnp.bfloat16),
            pltpu.VMEM((sets, rows, 4 * panel), jnp.bfloat16),
            pltpu.VMEM((nct, 4, panel, cw), jnp.bfloat16),
            pltpu.VMEM((nct, rows, cw), jnp.int16),
            pltpu.VMEM((nct, GROUPS, cw), jnp.float32),
            pltpu.VMEM((nct, rows, cw), jnp.int16),
            pltpu.VMEM((nct, GROUPS, cw), jnp.float32),
            dma, dma, dma, dma((len(orients),)), dma((len(orients),)),
            dma((3,)), dma((3,)), dma((3,)), dma((3,)), dma((4,)), dma((4,)),
        ] + [dma((nct,))] * 11,
        compiler_params=pltpu.CompilerParams(
            collective_id=0, has_side_effects=True, vmem_limit_bytes=48 * 2**20),
        cost_estimate=pl.CostEstimate(
            flops=2 * rows * 4 * panel * width, bytes_accessed=8 * rows * width, transcendentals=0),
    )(counts, owner, tokens.T, weight)
    return pl.pallas_call(
        functools.partial(store_kernel, parts),
        out_shape=jax.ShapeDtypeStruct((rows, width), jnp.float32),
        in_specs=[pl.BlockSpec(memory_space=pltpu.VMEM)],
        out_specs=pl.BlockSpec(memory_space=pl.ANY),
        scratch_shapes=[dma((parts,))],
        compiler_params=pltpu.CompilerParams(vmem_limit_bytes=16 * 2**20),
    )(pltpu.with_memory_space_constraint(blocks, pltpu.VMEM))


def solution(mesh):
    in_specs = (P("row", "col"), P("row", "col"), P("row"), P())
    out_specs = P("row", "col")
    planned = dict(mesh.shape) == {"row": 4, "col": 8}
    return jax.shard_map(
        per_device if planned else per_device_general,
        mesh=mesh, in_specs=in_specs, out_specs=out_specs, check_vma=False,
    )
```
